128 devices in a mesh: freq: 32 (over z, y, core), row: 2 (over x_hi), col: 2 (over x_lo).
Axes of the slice: x: 4 (x_hi: 2, x_lo: 2; x = x_hi * 2 + x_lo), y: 4, z: 4, core: 2. Of those that a mesh axis runs over, the one named last changes fastest.
Arguments:
- signals: bfloat16 [2000, 2048, 320], P(None, ('freq', 'row', 'col')), may hold values from -16 to 16
- block_of: int32 [2048], replicated, may hold values from 0 to 1, as said below
- kept_bins: int32 [32], replicated, may hold values from 0 to 127, as said below
Outputs:
- cross_real: bfloat16 [32, 2048, 2048], P('freq', 'row', 'col')
- cross_imag: bfloat16 [32, 2048, 2048], P('freq', 'row', 'col')
The draws below stay inside these ranges and needn't reach their ends.
Inputs may be any that keep to these rules, and one draw needn't show every extreme that they name: `block_of`: exactly 1024 stations have each of the two values. `kept_bins`: distinct values.
All inputs are finite; a program needn't handle non-finite values.
Results may differ from the reference program's by a relative error of at most 0.0066.
Values may be sent and summed in bfloat16 or wider, within the bound.
No kernel may reach another device: no remote copies, remote signals or barrier semaphores. Data moves between devices by JAX's collectives and lax.ppermute only.
A program may use at most 128 MiB of HBM per device.

```python
import math
import jax
import jax.numpy as jnp
from jax import lax

STATIONS = 2048
SAMPLES = 2000
FIRST = 40
CAND = 128
WINDOWS = 320
KEPT = 32


def draw_signals(key, part):
    key = jax.random.fold_in(key, 11)
    subkeys = jax.random.split(key, 5)
    shape_full = (SAMPLES, STATIONS, WINDOWS)
    station_noise = jnp.clip(jax.random.normal(subkeys[0], shape_full), -6.0, 6.0)
    common_weight = 0.5
    common = jnp.clip(jax.random.normal(subkeys[1], (SAMPLES, 1, WINDOWS)), -6.0, 6.0)
    coupling = jax.random.uniform(subkeys[2], (1, STATIONS, 1), minval=0.3, maxval=1.0)
    total = station_noise + common_weight * coupling * common
    line_bins = jax.random.randint(subkeys[3], (4,), 0, CAND) + FIRST
    sample_index = jnp.arange(SAMPLES, dtype=jnp.int32)
    for line_number in range(4):
        line_key = jax.random.fold_in(subkeys[4], line_number)
        amp_key, phase_key = jax.random.split(line_key)
        line_amp = jax.random.uniform(amp_key, (1, STATIONS, 1), minval=0.02, maxval=0.2)
        line_phase = jax.random.uniform(phase_key, (1, STATIONS, WINDOWS), minval=-math.pi, maxval=math.pi)
        phase_turns = sample_index * line_bins[line_number] % SAMPLES
        phase_angle = phase_turns.astype(jnp.float32) * (2.0 * math.pi / SAMPLES)
        total = total + line_amp * jnp.cos(phase_angle[:, None, None] + line_phase)
    return total.astype(jnp.bfloat16)


def draw_block_of(key, part):
    key = jax.random.fold_in(key, 12)
    shuffled = jax.random.permutation(key, STATIONS)
    return (shuffled >= STATIONS // 2).astype(jnp.int32)


def draw_kept_bins(key, part):
    key = jax.random.fold_in(key, 13)
    first_key, second_key = jax.random.split(key)
    middle = jax.random.permutation(first_key, CAND - 2)[:KEPT - 2] + 1
    ends = jnp.array([0, CAND - 1], dtype=jnp.int32)
    chosen = jnp.concatenate([ends, middle.astype(jnp.int32)])
    return jax.random.permutation(second_key, chosen).astype(jnp.int32)


def setup_inputs(seed: int = 0) -> dict:
    seeds = jax.random.split(jax.random.key(seed), 4)
    return {
        "signals": draw_signals(jax.random.fold_in(seeds[3], 71), 0),
        "block_of": draw_block_of(jax.random.fold_in(seeds[3], 71), 0),
        "kept_bins": draw_kept_bins(jax.random.fold_in(seeds[3], 71), 0),
    }


def build_table():
    sample_index = jnp.arange(SAMPLES, dtype=jnp.int32)
    bin_index = jnp.arange(CAND, dtype=jnp.int32) + FIRST
    phase_turns = sample_index[:, None] * bin_index[None, :] % SAMPLES
    phase_angle = phase_turns.astype(jnp.float32) * (2.0 * math.pi / SAMPLES)
    return jnp.concatenate([jnp.cos(phase_angle), -jnp.sin(phase_angle)], axis=1).astype(jnp.bfloat16)

def reference(signals, block_of, kept_bins):
    dft_table = build_table()
    flat_signals = signals.reshape(SAMPLES, STATIONS * WINDOWS)
    spectra = jnp.dot(dft_table.T, flat_signals, preferred_element_type=jnp.float32)
    real_part = spectra[:CAND]
    imag_part = spectra[CAND:]
    band_power = lax.optimization_barrier(jnp.mean(real_part * real_part + imag_part * imag_part, axis=0))
    whiten_scale = 1.0 / jnp.sqrt(band_power + 1e-06)
    kept_real = jnp.take(real_part, kept_bins, axis=0) * whiten_scale
    kept_imag = jnp.take(imag_part, kept_bins, axis=0) * whiten_scale
    panels = jnp.concatenate([kept_real.reshape(KEPT, STATIONS, WINDOWS), kept_imag.reshape(KEPT, STATIONS, WINDOWS)], axis=2).astype(jnp.bfloat16)
    half_count = STATIONS // 2
    order_zero = jnp.nonzero(block_of == 0, size=half_count)[0].astype(jnp.int32)
    order_one = jnp.nonzero(block_of == 1, size=half_count)[0].astype(jnp.int32)
    station_order = jnp.concatenate([order_zero, order_one]).astype(jnp.int32)
    ordered = jnp.take(panels, station_order, axis=1)
    contract = (((1,), (1,)), ((), ()))

    def cross_one_bin(panel_rows):
        twisted = jnp.concatenate([panel_rows[:, WINDOWS:], -panel_rows[:, :WINDOWS]], axis=1)
        real_sum = lax.dot_general(panel_rows, panel_rows, contract, preferred_element_type=jnp.float32)
        imag_sum = lax.dot_general(twisted, panel_rows, contract, preferred_element_type=jnp.float32)
        return ((real_sum / WINDOWS).astype(jnp.bfloat16), (imag_sum / WINDOWS).astype(jnp.bfloat16))
    cross_real, cross_imag = lax.map(cross_one_bin, ordered)
    return (cross_real, cross_imag)
```

```python
import math

import jax
import jax.numpy as jnp
import numpy as np
from jax import lax
from jax.experimental import pallas as pl
from jax.experimental.pallas import tpu as pltpu
from jax.sharding import PartitionSpec as P

STATIONS = 2048
SAMPLES = 2000
FIRST = 40
CAND = 128
WINDOWS = 320
KEPT = 32
LOCAL = 16
WIDE = 2 * WINDOWS
COPIES = 4
HALF = STATIONS // 2
GROUP = 256
GROUPS = STATIONS // GROUP
WINDOW = GROUP + 16
STEP_STATIONS = 2
ROW_TILE = 256
LANES = 128
NT = (((1,), (1,)), ((), ()))


def build_table():
    turns = np.arange(SAMPLES)[:, None] * (np.arange(CAND) + FIRST)[None, :] % SAMPLES
    angle = turns.astype(np.float32) * np.float32(2.0 * math.pi / SAMPLES)
    return np.concatenate([np.cos(angle), -np.sin(angle)], axis=1).astype(jnp.bfloat16)


def whiten_kernel(kept_ref, table_ref, signals_ref, out_ref, pick, rows):
    step = pl.program_id(0)

    @pl.when(step == 0)
    def _():
        lane = lax.broadcasted_iota(jnp.int32, (1, 2 * CAND), 1)
        for b in range(KEPT):
            bin_index = kept_ref[b]
            pick[pl.ds(b, 1), :] = (lane == bin_index).astype(jnp.float32)
            pick[pl.ds(KEPT + b, 1), :] = (lane == CAND + bin_index).astype(jnp.float32)

    flat = signals_ref[...].reshape(STEP_STATIONS * WINDOWS, SAMPLES)
    spectra = jnp.dot(flat, table_ref[...], preferred_element_type=jnp.float32)
    band_power = jnp.sum(spectra * spectra, axis=1, keepdims=True) * (1.0 / CAND)
    whitened = (spectra * lax.rsqrt(band_power + 1e-06)).astype(jnp.bfloat16)
    picked = lax.dot_general(
        pick[...].astype(jnp.bfloat16), whitened, NT, preferred_element_type=jnp.float32
    )
    for j in range(STEP_STATIONS):
        mine = picked[:, j * WINDOWS : (j + 1) * WINDOWS]
        both = jnp.concatenate([mine[:KEPT], mine[KEPT:]], axis=1)
        place = pl.Slice(step * STEP_STATIONS + j, KEPT, LOCAL)
        for t in range(WIDE // LANES):
            rows[t, place, :] = both[:, t * LANES : (t + 1) * LANES]

    @pl.when(step == pl.num_programs(0) - 1)
    def _():
        for t in range(WIDE // LANES):
            panels = rows[t].reshape(KEPT, LOCAL, LANES).astype(jnp.bfloat16)
            for j in range(COPIES):
                out_ref[:, j, :, t * LANES : (t + 1) * LANES] = panels


def whiten(signals, kept_bins):
    return pl.pallas_call(
        whiten_kernel,
        grid=(LOCAL // STEP_STATIONS,),
        in_specs=[
            pl.BlockSpec(memory_space=pltpu.SMEM),
            pl.BlockSpec((SAMPLES, 2 * CAND), lambda i: (0, 0)),
            pl.BlockSpec((STEP_STATIONS, WINDOWS, SAMPLES), lambda i: (i, 0, 0)),
        ],
        out_specs=pl.BlockSpec((KEPT, COPIES, LOCAL, WIDE), lambda i: (0, 0, 0, 0)),
        out_shape=jax.ShapeDtypeStruct((KEPT, COPIES, LOCAL, WIDE), jnp.bfloat16),
        scratch_shapes=[
            pltpu.VMEM((2 * KEPT, 2 * CAND), jnp.float32),
            pltpu.VMEM((WIDE // LANES, KEPT * LOCAL, LANES), jnp.float32),
        ],
        compiler_params=pltpu.CompilerParams(vmem_limit_bytes=48 * 1024 * 1024),
        name="whiten",
    )(kept_bins, build_table(), jnp.transpose(signals, (1, 2, 0)))


def places(block_of, which):
    member = (block_of == which).reshape(GROUPS, GROUP)
    index = np.arange(GROUP)
    before = jnp.asarray((index[:, None] < index[None, :]).astype(jnp.bfloat16))
    ones = member.astype(jnp.bfloat16)
    rank = jnp.dot(ones, before, preferred_element_type=jnp.float32).astype(jnp.int32)
    count = jnp.sum(member.astype(jnp.int32), axis=1)
    group = np.arange(GROUPS)
    earlier = jnp.asarray((group[:, None] < group[None, :]).astype(np.int32))
    offset = jnp.sum(count[:, None] * earlier, axis=0)
    shift = offset % 16
    target = jnp.where(member, rank + shift[:, None], -1)
    return target, offset - shift


def cross_kernel(base_ref, target_ref, panel_ref, real_ref, imag_ref, sorted_rows, sorted_cols):
    step = pl.program_id(0)

    @pl.when(step == 0)
    def _():
        place = lax.broadcasted_iota(jnp.int32, (WINDOW, GROUP), 0)
        for side, dest in ((0, sorted_rows), (1, sorted_cols)):
            dest[0:16, :] = jnp.zeros((16, WIDE), jnp.bfloat16)
            for g in range(GROUPS):
                hit = (place == target_ref[side, g : g + 1, :]).astype(jnp.bfloat16)
                moved = jnp.dot(
                    hit, panel_ref[g * GROUP : (g + 1) * GROUP, :], preferred_element_type=jnp.float32
                ).astype(jnp.bfloat16)
                base = pl.multiple_of(base_ref[side, g], 16)
                dest[pl.ds(base, 16), :] += moved[:16]
                dest[pl.ds(pl.multiple_of(base + 16, 16), GROUP), :] = moved[16:]

    rows = sorted_rows[pl.ds(pl.multiple_of(step * ROW_TILE, ROW_TILE), ROW_TILE), :]
    twisted = jnp.concatenate([rows[:, WINDOWS:], -rows[:, :WINDOWS]], axis=1)
    cols = sorted_cols[0:HALF, :]
    scale = 1.0 / WINDOWS
    real_sum = lax.dot_general(rows, cols, NT, preferred_element_type=jnp.float32)
    real_ref[0] = (real_sum * scale).astype(jnp.bfloat16)
    imag_sum = lax.dot_general(twisted, cols, NT, preferred_element_type=jnp.float32)
    imag_ref[0] = (imag_sum * scale).astype(jnp.bfloat16)


def cross(base, target, panel):
    block = pl.BlockSpec((1, ROW_TILE, HALF), lambda i: (0, i, 0))
    shape = jax.ShapeDtypeStruct((1, HALF, HALF), jnp.bfloat16)
    return pl.pallas_call(
        cross_kernel,
        grid=(HALF // ROW_TILE,),
        in_specs=[
            pl.BlockSpec(memory_space=pltpu.SMEM),
            pl.BlockSpec((2, GROUPS, GROUP), lambda i: (0, 0, 0)),
            pl.BlockSpec((STATIONS, WIDE), lambda i: (0, 0)),
        ],
        out_specs=[block, block],
        out_shape=[shape, shape],
        scratch_shapes=[
            pltpu.VMEM((HALF + WINDOW, WIDE), jnp.bfloat16),
            pltpu.VMEM((HALF + WINDOW, WIDE), jnp.bfloat16),
        ],
        compiler_params=pltpu.CompilerParams(vmem_limit_bytes=48 * 1024 * 1024),
        name="cross",
    )(base, target, panel)


def on_device(signals, block_of, kept_bins):
    panels = whiten(signals, kept_bins).reshape(KEPT * COPIES, LOCAL, WIDE)
    relaid = lax.all_to_all(
        panels, ("freq", "row", "col"), split_axis=0, concat_axis=0, tiled=True
    )
    row_target, row_base = places(block_of, lax.axis_index("row"))
    col_target, col_base = places(block_of, lax.axis_index("col"))
    base = jnp.stack([row_base, col_base])
    target = jnp.stack([row_target, col_target])
    cross_real, cross_imag = cross(base, target, relaid.reshape(STATIONS, WIDE))
    return (cross_real, cross_imag)


def solution(mesh):
    return jax.shard_map(
        on_device,
        mesh=mesh,
        in_specs=(P(None, ("freq", "row", "col"), None), P(), P()),
        out_specs=(P("freq", "row", "col"), P("freq", "row", "col")),
        check_vma=False,
    )
```

```python
import math

import jax
import jax.numpy as jnp
import numpy as np
from jax import lax
from jax.experimental import pallas as pl
from jax.experimental.pallas import tpu as pltpu
from jax.sharding import PartitionSpec as P

STATIONS = 2048
SAMPLES = 2000
FIRST = 40
CAND = 128
WINDOWS = 320
KEPT = 32
LOCAL = 16
WIDE = 2 * WINDOWS
COPIES = 4
HALF = STATIONS // 2
GROUP = 256
GROUPS = STATIONS // GROUP
WINDOW = GROUP + 16
STEP_STATIONS = 4
DEPTH = 2
ROW_TILE = 256
LANES = 128
NT = (((1,), (1,)), ((), ()))


def build_table():
    turns = np.arange(SAMPLES)[:, None] * (np.arange(CAND) + FIRST)[None, :] % SAMPLES
    angle = turns.astype(np.float32) * np.float32(2.0 * math.pi / SAMPLES)
    return np.concatenate([np.cos(angle), -np.sin(angle)], axis=1).astype(jnp.bfloat16)


def bin_order(kept, chosen):
    lane = lax.broadcasted_iota(jnp.int32, (1, CAND), 1)
    for b in range(KEPT):
        chosen[pl.ds(b, 1), :] = (lane == kept[b]).astype(jnp.float32)
    first = chosen[...]
    other = 1.0 - jnp.sum(first, axis=0, keepdims=True)
    square = (CAND, CAND)
    before = lax.broadcasted_iota(jnp.int32, square, 0) < lax.broadcasted_iota(jnp.int32, square, 1)
    rank = jnp.dot(
        jnp.broadcast_to(other, (8, CAND)).astype(jnp.bfloat16),
        before.astype(jnp.bfloat16),
        preferred_element_type=jnp.float32,
    )[:1]
    place = jnp.where(other > 0.5, rank, -1.0).astype(jnp.int32)
    rest = lax.broadcasted_iota(jnp.int32, (CAND - KEPT, CAND), 0) == place
    rest = rest.astype(jnp.float32)
    none_first, none_rest = jnp.zeros_like(first), jnp.zeros_like(rest)
    halves = ((first, none_first), (none_first, first), (rest, none_rest), (none_rest, rest))
    order = jnp.concatenate([jnp.concatenate(pair, axis=1) for pair in halves], axis=0)
    return order.astype(jnp.bfloat16)


def whiten_kernel(
    kept_hbm,
    table_hbm,
    signals_hbm,
    out_hbm,
    kept,
    table,
    signals,
    chosen,
    spectra_of_last,
    rows,
    panels,
    small_sems,
    sems,
    out_sems,
):
    steps = LOCAL // STEP_STATIONS

    def fetch(i):
        span = pl.ds(i * STEP_STATIONS, STEP_STATIONS)
        return pltpu.make_async_copy(signals_hbm.at[span], signals.at[span], sems.at[i])

    kept_copy = pltpu.make_async_copy(kept_hbm, kept, small_sems.at[0])
    table_copy = pltpu.make_async_copy(table_hbm, table, small_sems.at[1])
    kept_copy.start()
    table_copy.start()
    for i in range(DEPTH):
        fetch(i).start()
    kept_copy.wait()
    order = bin_order(kept, chosen)
    table_copy.wait()
    table[...] = lax.dot_general(
        table[...], order, NT, preferred_element_type=jnp.float32
    ).astype(jnp.bfloat16)

    def finish(spectra, i):
        band_power = jnp.sum(spectra * spectra, axis=1, keepdims=True) * (1.0 / CAND)
        scale = lax.rsqrt(band_power + 1e-06)
        picked = (spectra[:, :LANES] * scale).astype(jnp.bfloat16).T[: 2 * KEPT]
        picked = picked.astype(jnp.float32)
        for j in range(STEP_STATIONS):
            mine = picked[:, j * WINDOWS : (j + 1) * WINDOWS]
            both = jnp.concatenate([mine[:KEPT], mine[KEPT:]], axis=1)
            place = pl.Slice(i * STEP_STATIONS + j, KEPT, LOCAL)
            for t in range(WIDE // LANES):
                rows[t, place, :] = both[:, t * LANES : (t + 1) * LANES]

    spectra_of_last[...] = jnp.zeros_like(spectra_of_last)

    def body(i, carry):
        fetch(i).wait()

        @pl.when(i + DEPTH < steps)
        def _():
            fetch(i + DEPTH).start()

        finish(spectra_of_last[...], jnp.maximum(i - 1, 0))
        flat = signals[pl.ds(i * STEP_STATIONS, STEP_STATIONS)]
        flat = flat.reshape(STEP_STATIONS * WINDOWS, SAMPLES)
        spectra_of_last[...] = jnp.dot(flat, table[...], preferred_element_type=jnp.float32)
        return carry

    lax.fori_loop(0, steps, body, 0)
    finish(spectra_of_last[...], steps - 1)

    def send(t, j):
        lanes = pl.ds(t * LANES, LANES)
        return pltpu.make_async_copy(
            panels.at[t], out_hbm.at[:, j, :, lanes], out_sems.at[t, j]
        )

    for t in range(WIDE // LANES):
        panels[t] = rows[t].reshape(KEPT, LOCAL, LANES).astype(jnp.bfloat16)
        for j in range(COPIES):
            send(t, j).start()
    for t in range(WIDE // LANES):
        for j in range(COPIES):
            send(t, j).wait()


def whiten(signals, kept_bins):
    hbm = pl.BlockSpec(memory_space=pltpu.HBM)
    return pl.pallas_call(
        whiten_kernel,
        in_specs=[hbm, hbm, hbm],
        out_specs=hbm,
        out_shape=jax.ShapeDtypeStruct((KEPT, COPIES, LOCAL, WIDE), jnp.bfloat16),
        scratch_shapes=[
            pltpu.SMEM((KEPT,), jnp.int32),
            pltpu.VMEM((SAMPLES, 2 * CAND), jnp.bfloat16),
            pltpu.VMEM((LOCAL, WINDOWS, SAMPLES), jnp.bfloat16),
            pltpu.VMEM((KEPT, CAND), jnp.float32),
            pltpu.VMEM((STEP_STATIONS * WINDOWS, 2 * CAND), jnp.float32),
            pltpu.VMEM((WIDE // LANES, KEPT * LOCAL, LANES), jnp.float32),
            pltpu.VMEM((WIDE // LANES, KEPT, LOCAL, LANES), jnp.bfloat16),
            pltpu.SemaphoreType.DMA((2,)),
            pltpu.SemaphoreType.DMA((LOCAL // STEP_STATIONS,)),
            pltpu.SemaphoreType.DMA((WIDE // LANES, COPIES)),
        ],
        compiler_params=pltpu.CompilerParams(vmem_limit_bytes=60 * 1024 * 1024),
        name="whiten",
    )(kept_bins, build_table(), jnp.transpose(signals, (1, 2, 0)))


def places(block_of, which):
    member = (block_of == which).reshape(GROUPS, GROUP)
    index = np.arange(GROUP)
    before = jnp.asarray((index[:, None] < index[None, :]).astype(jnp.bfloat16))
    ones = member.astype(jnp.bfloat16)
    rank = jnp.dot(ones, before, preferred_element_type=jnp.float32).astype(jnp.int32)
    count = jnp.sum(member.astype(jnp.int32), axis=1)
    group = np.arange(GROUPS)
    earlier = jnp.asarray((group[:, None] < group[None, :]).astype(np.int32))
    offset = jnp.sum(count[:, None] * earlier, axis=0)
    shift = offset % 16
    target = jnp.where(member, rank + shift[:, None], -1)
    return target, offset - shift


def cross_kernel(
    base_ref, target_ref, panel_ref, real_hbm, imag_hbm, sorted_rows, sorted_cols, out, sems
):
    place = lax.broadcasted_iota(jnp.int32, (WINDOW, GROUP), 0)
    sides = (sorted_rows, sorted_cols)
    for dest in sides:
        dest[0:16, :] = jnp.zeros((16, WIDE), jnp.bfloat16)
    for g in range(GROUPS):
        group = panel_ref[g * GROUP : (g + 1) * GROUP, :]
        for side, dest in enumerate(sides):
            hit = (place == target_ref[side, g : g + 1, :]).astype(jnp.bfloat16)
            moved = jnp.dot(hit, group, preferred_element_type=jnp.float32).astype(jnp.bfloat16)
            base = pl.multiple_of(base_ref[side, g], 16)
            dest[pl.ds(base, 16), :] += moved[:16]
            dest[pl.ds(pl.multiple_of(base + 16, 16), GROUP), :] = moved[16:]

    cols = sorted_cols[0:HALF, :]
    scale = 1.0 / WINDOWS

    def send(i, part):
        span = pl.ds(i * ROW_TILE, ROW_TILE)
        dest = (real_hbm, imag_hbm)[part].at[0, span]
        return pltpu.make_async_copy(out.at[i, part], dest, sems.at[i, part])

    for i in range(HALF // ROW_TILE):
        rows = sorted_rows[i * ROW_TILE : (i + 1) * ROW_TILE, :]
        twisted = jnp.concatenate([rows[:, WINDOWS:], -rows[:, :WINDOWS]], axis=1)
        for part, left in enumerate((rows, twisted)):
            total = lax.dot_general(left, cols, NT, preferred_element_type=jnp.float32)
            out[i, part] = (total * scale).astype(jnp.bfloat16)
            send(i, part).start()
    for i in range(HALF // ROW_TILE):
        for part in range(2):
            send(i, part).wait()


def cross(base, target, panel):
    shape = jax.ShapeDtypeStruct((1, HALF, HALF), jnp.bfloat16)
    hbm = pl.BlockSpec(memory_space=pltpu.HBM)
    vmem = pl.BlockSpec(memory_space=pltpu.VMEM)
    return pl.pallas_call(
        cross_kernel,
        in_specs=[pl.BlockSpec(memory_space=pltpu.SMEM), vmem, vmem],
        out_specs=[hbm, hbm],
        out_shape=[shape, shape],
        scratch_shapes=[
            pltpu.VMEM((HALF + WINDOW, WIDE), jnp.bfloat16),
            pltpu.VMEM((HALF + WINDOW, WIDE), jnp.bfloat16),
            pltpu.VMEM((HALF // ROW_TILE, 2, ROW_TILE, HALF), jnp.bfloat16),
            pltpu.SemaphoreType.DMA((HALF // ROW_TILE, 2)),
        ],
        compiler_params=pltpu.CompilerParams(vmem_limit_bytes=32 * 1024 * 1024),
        name="cross",
    )(base, target, panel)


def on_device(signals, block_of, kept_bins):
    panels = whiten(signals, kept_bins).reshape(KEPT * COPIES, LOCAL, WIDE)
    relaid = lax.all_to_all(
        panels, ("freq", "row", "col"), split_axis=0, concat_axis=0, tiled=True
    )
    row_target, row_base = places(block_of, lax.axis_index("row"))
    col_target, col_base = places(block_of, lax.axis_index("col"))
    base = jnp.stack([row_base, col_base])
    target = jnp.stack([row_target, col_target])
    cross_real, cross_imag = cross(base, target, relaid.reshape(STATIONS, WIDE))
    return (cross_real, cross_imag)


def solution(mesh):
    return jax.shard_map(
        on_device,
        mesh=mesh,
        in_specs=(P(None, ("freq", "row", "col"), None), P(), P()),
        out_specs=(P("freq", "row", "col"), P("freq", "row", "col")),
        check_vma=False,
    )
```

```python
import math

import jax
import jax.numpy as jnp
import numpy as np
from jax import lax
from jax.experimental import pallas as pl
from jax.experimental.pallas import tpu as pltpu
from jax.sharding import PartitionSpec as P

STATIONS = 2048
SAMPLES = 2000
FIRST = 40
CAND = 128
WINDOWS = 320
KEPT = 32
LOCAL = 16
WIDE = 2 * WINDOWS
COPIES = 4
HALF = STATIONS // 2
GROUP = 256
GROUPS = STATIONS // GROUP
WINDOW = GROUP + 16
PAIR = GROUP + 48
SPAN = 64
STEPS = WINDOWS // SPAN
DEPTH = 2
ROW_TILE = 256
LANES = 128
NT = (((1,), (1,)), ((), ()))


def build_table():
    turns = np.arange(SAMPLES)[:, None] * (np.arange(CAND) + FIRST)[None, :] % SAMPLES
    angle = turns.astype(np.float32) * np.float32(2.0 * math.pi / SAMPLES)
    return np.concatenate([np.cos(angle), -np.sin(angle)], axis=1).astype(jnp.bfloat16)


def bin_order(kept, chosen):
    lane = lax.broadcasted_iota(jnp.int32, (1, CAND), 1)
    for b in range(KEPT):
        chosen[pl.ds(b, 1), :] = (lane == kept[b]).astype(jnp.float32)
    first = chosen[...]
    other = 1.0 - jnp.sum(first, axis=0, keepdims=True)
    square = (CAND, CAND)
    before = lax.broadcasted_iota(jnp.int32, square, 0) < lax.broadcasted_iota(jnp.int32, square, 1)
    rank = jnp.dot(
        jnp.broadcast_to(other, (8, CAND)).astype(jnp.bfloat16),
        before.astype(jnp.bfloat16),
        preferred_element_type=jnp.float32,
    )[:1]
    place = jnp.where(other > 0.5, rank, -1.0).astype(jnp.int32)
    rest = lax.broadcasted_iota(jnp.int32, (CAND - KEPT, CAND), 0) == place
    rest = rest.astype(jnp.float32)
    none_first, none_rest = jnp.zeros_like(first), jnp.zeros_like(rest)
    halves = ((first, none_first), (none_first, first), (rest, none_rest), (none_rest, rest))
    order = jnp.concatenate([jnp.concatenate(pair, axis=1) for pair in halves], axis=0)
    return order.astype(jnp.bfloat16)


def whiten_kernel(
    kept_hbm,
    table_hbm,
    signals_hbm,
    out_hbm,
    kept,
    table,
    signals,
    chosen,
    spectra_of_last,
    rows,
    panels,
    small_sems,
    sems,
    out_sems,
):
    def fetch(i):
        span = pl.ds(pl.multiple_of(i * SPAN, SPAN), SPAN)
        return pltpu.make_async_copy(signals_hbm.at[:, span], signals.at[i], sems.at[i])

    def send(i, j):
        lanes = pl.ds(pl.multiple_of(i * LANES, LANES), LANES)
        return pltpu.make_async_copy(
            panels.at[i], out_hbm.at[:, j, :, lanes], out_sems.at[i, j]
        )

    kept_copy = pltpu.make_async_copy(kept_hbm, kept, small_sems.at[0])
    table_copy = pltpu.make_async_copy(table_hbm, table, small_sems.at[1])
    kept_copy.start()
    table_copy.start()
    for i in range(DEPTH):
        fetch(i).start()
    kept_copy.wait()
    order = bin_order(kept, chosen)
    table_copy.wait()
    table[...] = lax.dot_general(
        table[...], order, NT, preferred_element_type=jnp.float32
    ).astype(jnp.bfloat16)
    low = lax.broadcasted_iota(jnp.int32, (KEPT, LANES), 1) < SPAN

    def finish(spectra, i):
        band_power = jnp.sum(spectra * spectra, axis=1, keepdims=True) * (1.0 / CAND)
        scale = lax.rsqrt(band_power + 1e-06)
        picked = (spectra[:, :LANES] * scale).astype(jnp.bfloat16).T[: 2 * KEPT]
        picked = picked.astype(jnp.float32)
        for pair in range(LOCAL // 2):
            real = picked[:KEPT, pair * LANES : (pair + 1) * LANES]
            imag = picked[KEPT:, pair * LANES : (pair + 1) * LANES]
            even = jnp.where(low, real, pltpu.roll(imag, SPAN, 1))
            odd = jnp.where(low, pltpu.roll(real, SPAN, 1), imag)
            rows[pl.Slice(2 * pair, KEPT, LOCAL), :] = even
            rows[pl.Slice(2 * pair + 1, KEPT, LOCAL), :] = odd
        panels[i] = rows[...].reshape(KEPT, LOCAL, LANES).astype(jnp.bfloat16)

    spectra_of_last[...] = jnp.zeros_like(spectra_of_last)

    def body(i, carry):
        fetch(i).wait()

        @pl.when(i + DEPTH < STEPS)
        def _():
            fetch(i + DEPTH).start()

        finish(spectra_of_last[...], jnp.maximum(i - 1, 0))
        flat = signals[i].reshape(LOCAL * SPAN, SAMPLES)
        spectra_of_last[...] = jnp.dot(flat, table[...], preferred_element_type=jnp.float32)

        @pl.when(i > 0)
        def _():
            for j in range(COPIES):
                send(i - 1, j).start()

        return carry

    lax.fori_loop(0, STEPS, body, 0)
    finish(spectra_of_last[...], STEPS - 1)
    for j in range(COPIES):
        send(STEPS - 1, j).start()
    for i in range(STEPS):
        for j in range(COPIES):
            send(i, j).wait()


def whiten(signals, kept_bins):
    hbm = pl.BlockSpec(memory_space=pltpu.HBM)
    return pl.pallas_call(
        whiten_kernel,
        in_specs=[hbm, hbm, hbm],
        out_specs=hbm,
        out_shape=jax.ShapeDtypeStruct((KEPT, COPIES, LOCAL, WIDE), jnp.bfloat16),
        scratch_shapes=[
            pltpu.SMEM((KEPT,), jnp.int32),
            pltpu.VMEM((SAMPLES, 2 * CAND), jnp.bfloat16),
            pltpu.VMEM((STEPS, LOCAL, SPAN, SAMPLES), jnp.bfloat16),
            pltpu.VMEM((KEPT, CAND), jnp.float32),
            pltpu.VMEM((LOCAL * SPAN, 2 * CAND), jnp.float32),
            pltpu.VMEM((KEPT * LOCAL, LANES), jnp.float32),
            pltpu.VMEM((STEPS, KEPT, LOCAL, LANES), jnp.bfloat16),
            pltpu.SemaphoreType.DMA((2,)),
            pltpu.SemaphoreType.DMA((STEPS,)),
            pltpu.SemaphoreType.DMA((STEPS, COPIES)),
        ],
        compiler_params=pltpu.CompilerParams(vmem_limit_bytes=60 * 1024 * 1024),
        name="whiten",
    )(kept_bins, build_table(), jnp.transpose(signals, (1, 2, 0)))


def ranks(block_of, which):
    member = (block_of == which).reshape(GROUPS, GROUP)
    index = np.arange(GROUP)
    before = jnp.asarray((index[:, None] < index[None, :]).astype(jnp.bfloat16))
    ones = member.astype(jnp.bfloat16)
    rank = jnp.dot(ones, before, preferred_element_type=jnp.float32).astype(jnp.int32)
    count = jnp.sum(member.astype(jnp.int32), axis=1)
    group = np.arange(GROUPS)
    earlier = jnp.asarray((group[:, None] < group[None, :]).astype(np.int32))
    offset = jnp.sum(count[:, None] * earlier, axis=0)
    return member, rank, count, offset


def places(block_of, row, col):
    member, rank, count, offset = ranks(block_of, row)
    col_member, col_rank, _, col_offset = ranks(block_of, col)
    shift, col_shift = offset % 16, col_offset % 16
    second = jnp.where(row == col, 0, (shift + count) // 16 * 16 + 16)
    col_target = jnp.where(col_member, col_rank + (second + col_shift)[:, None], -1)
    target = jnp.where(member, rank + shift[:, None], col_target)
    return target, jnp.stack([offset - shift, col_offset - col_shift, second])


def cross_kernel(
    base_ref, target_ref, panel_ref, real_hbm, imag_hbm, sorted_rows, sorted_cols, both, out, sems
):
    place = lax.broadcasted_iota(jnp.int32, (PAIR, GROUP), 0)
    sides = (sorted_rows, sorted_cols)
    for dest in sides:
        dest[0:16, :] = jnp.zeros((16, WIDE), jnp.bfloat16)
    both[:, PAIR:, :] = jnp.zeros((2, WINDOW, WIDE), jnp.bfloat16)
    for g in range(GROUPS):
        group = panel_ref[g * GROUP : (g + 1) * GROUP, :]
        hit = (place == target_ref[g : g + 1, :]).astype(jnp.bfloat16)
        slot = g % 2
        both[slot, 0:PAIR, :] = jnp.dot(hit, group, preferred_element_type=jnp.float32).astype(
            jnp.bfloat16
        )
        for side, dest in enumerate(sides):
            start = pl.multiple_of(base_ref[2, g], 16) if side else 0
            base = pl.multiple_of(base_ref[side, g], 16)
            dest[pl.ds(base, 16), :] += both[slot, pl.ds(start, 16), :]
            dest[pl.ds(pl.multiple_of(base + 16, 16), GROUP), :] = both[
                slot, pl.ds(pl.multiple_of(start + 16, 16), GROUP), :
            ]

    cols = sorted_cols[0:HALF, :]
    scale = 1.0 / WINDOWS

    def send(i, part):
        span = pl.ds(i * ROW_TILE, ROW_TILE)
        dest = (real_hbm, imag_hbm)[part].at[0, span]
        return pltpu.make_async_copy(out.at[i, part], dest, sems.at[i, part])

    for i in range(HALF // ROW_TILE):
        rows = sorted_rows[i * ROW_TILE : (i + 1) * ROW_TILE, :]
        halves = [rows[:, k * SPAN : (k + 1) * SPAN] for k in range(2 * STEPS)]
        turned = [(halves[2 * k + 1], -halves[2 * k]) for k in range(STEPS)]
        twisted = jnp.concatenate([half for pair in turned for half in pair], axis=1)
        for part, left in enumerate((rows, twisted)):
            total = lax.dot_general(left, cols, NT, preferred_element_type=jnp.float32)
            out[i, part] = (total * scale).astype(jnp.bfloat16)
            send(i, part).start()
    for i in range(HALF // ROW_TILE):
        for part in range(2):
            send(i, part).wait()


def cross(base, target, panel):
    shape = jax.ShapeDtypeStruct((1, HALF, HALF), jnp.bfloat16)
    hbm = pl.BlockSpec(memory_space=pltpu.HBM)
    vmem = pl.BlockSpec(memory_space=pltpu.VMEM)
    return pl.pallas_call(
        cross_kernel,
        in_specs=[pl.BlockSpec(memory_space=pltpu.SMEM), vmem, vmem],
        out_specs=[hbm, hbm],
        out_shape=[shape, shape],
        scratch_shapes=[
            pltpu.VMEM((HALF + WINDOW, WIDE), jnp.bfloat16),
            pltpu.VMEM((HALF + WINDOW, WIDE), jnp.bfloat16),
            pltpu.VMEM((2, PAIR + WINDOW, WIDE), jnp.bfloat16),
            pltpu.VMEM((HALF // ROW_TILE, 2, ROW_TILE, HALF), jnp.bfloat16),
            pltpu.SemaphoreType.DMA((HALF // ROW_TILE, 2)),
        ],
        compiler_params=pltpu.CompilerParams(vmem_limit_bytes=32 * 1024 * 1024),
        name="cross",
    )(base, target, panel)


def on_device(signals, block_of, kept_bins):
    panels = whiten(signals, kept_bins).reshape(KEPT * COPIES, LOCAL, WIDE)
    relaid = lax.all_to_all(
        panels, ("freq", "row", "col"), split_axis=0, concat_axis=0, tiled=True
    )
    target, base = places(block_of, lax.axis_index("row"), lax.axis_index("col"))
    cross_real, cross_imag = cross(base, target, relaid.reshape(STATIONS, WIDE))
    return (cross_real, cross_imag)


def solution(mesh):
    return jax.shard_map(
        on_device,
        mesh=mesh,
        in_specs=(P(None, ("freq", "row", "col"), None), P(), P()),
        out_specs=(P("freq", "row", "col"), P("freq", "row", "col")),
        check_vma=False,
    )
```

```python
import math

import jax
import jax.numpy as jnp
import numpy as np
from jax import lax
from jax.experimental import pallas as pl
from jax.experimental.pallas import tpu as pltpu
from jax.sharding import PartitionSpec as P

STATIONS = 2048
SAMPLES = 2000
FIRST = 40
CAND = 128
WINDOWS = 320
KEPT = 32
LOCAL = 16
WIDE = 2 * WINDOWS
COPIES = 4
HALF = STATIONS // 2
GROUP = 256
GROUPS = STATIONS // GROUP
WINDOW = GROUP + 16
PAIR = GROUP + 48
SPAN = 64
STEPS = WINDOWS // SPAN
DEPTH = 2
ROW_TILE = 256
LANES = 128
NT = (((1,), (1,)), ((), ()))


def build_table():
    turns = np.arange(SAMPLES)[:, None] * (np.arange(CAND) + FIRST)[None, :] % SAMPLES
    angle = turns.astype(np.float32) * np.float32(2.0 * math.pi / SAMPLES)
    return np.concatenate([np.cos(angle), -np.sin(angle)], axis=1).astype(jnp.bfloat16)


def bin_order(kept, chosen):
    lane = lax.broadcasted_iota(jnp.int32, (1, CAND), 1)
    for b in range(KEPT):
        chosen[pl.ds(b, 1), :] = (lane == kept[b]).astype(jnp.float32)
    first = chosen[...]
    other = 1.0 - jnp.sum(first, axis=0, keepdims=True)
    square = (CAND, CAND)
    before = lax.broadcasted_iota(jnp.int32, square, 0) < lax.broadcasted_iota(jnp.int32, square, 1)
    rank = jnp.dot(
        jnp.broadcast_to(other, (8, CAND)).astype(jnp.bfloat16),
        before.astype(jnp.bfloat16),
        preferred_element_type=jnp.float32,
    )[:1]
    place = jnp.where(other > 0.5, rank, -1.0).astype(jnp.int32)
    rest = lax.broadcasted_iota(jnp.int32, (CAND - KEPT, CAND), 0) == place
    rest = rest.astype(jnp.float32)
    none_first, none_rest = jnp.zeros_like(first), jnp.zeros_like(rest)
    halves = ((first, none_first), (none_first, first), (rest, none_rest), (none_rest, rest))
    order = jnp.concatenate([jnp.concatenate(pair, axis=1) for pair in halves], axis=0)
    return order.astype(jnp.bfloat16)


def whiten_kernel(
    kept_hbm,
    table_hbm,
    signals_hbm,
    out_hbm,
    kept,
    table,
    signals,
    chosen,
    spectra_of_last,
    rows,
    panels,
    small_sems,
    sems,
    out_sems,
):
    def fetch(i):
        span = pl.ds(pl.multiple_of(i * SPAN, SPAN), SPAN)
        return pltpu.make_async_copy(signals_hbm.at[:, span], signals.at[i], sems.at[i])

    def send(i, j):
        lanes = pl.ds(pl.multiple_of(i * LANES, LANES), LANES)
        return pltpu.make_async_copy(
            panels.at[i], out_hbm.at[:, j, :, lanes], out_sems.at[i, j]
        )

    kept_copy = pltpu.make_async_copy(kept_hbm, kept, small_sems.at[0])
    table_copy = pltpu.make_async_copy(table_hbm, table, small_sems.at[1])
    kept_copy.start()
    table_copy.start()
    fetch(0).start()
    kept_copy.wait()
    order = bin_order(kept, chosen)
    table_copy.wait()
    fetch(1).start()
    table[...] = lax.dot_general(
        table[...], order, NT, preferred_element_type=jnp.float32
    ).astype(jnp.bfloat16)
    low = lax.broadcasted_iota(jnp.int32, (KEPT, LANES), 1) < SPAN

    def finish(spectra, i):
        band_power = jnp.sum(spectra * spectra, axis=1, keepdims=True) * (1.0 / CAND)
        scale = lax.rsqrt(band_power + 1e-06)
        picked = (spectra[:, :LANES] * scale).astype(jnp.bfloat16).T[: 2 * KEPT]
        picked = picked.astype(jnp.float32)
        for pair in range(LOCAL // 2):
            real = picked[:KEPT, pair * LANES : (pair + 1) * LANES]
            imag = picked[KEPT:, pair * LANES : (pair + 1) * LANES]
            even = jnp.where(low, real, pltpu.roll(imag, SPAN, 1))
            odd = jnp.where(low, pltpu.roll(real, SPAN, 1), imag)
            rows[pl.Slice(2 * pair, KEPT, LOCAL), :] = even
            rows[pl.Slice(2 * pair + 1, KEPT, LOCAL), :] = odd
        panels[i] = rows[...].reshape(KEPT, LOCAL, LANES).astype(jnp.bfloat16)

    spectra_of_last[...] = jnp.zeros_like(spectra_of_last)

    def body(i, carry):
        fetch(i).wait()

        @pl.when(i + DEPTH < STEPS)
        def _():
            fetch(i + DEPTH).start()

        finish(spectra_of_last[...], jnp.maximum(i - 1, 0))
        flat = signals[i].reshape(LOCAL * SPAN, SAMPLES)
        spectra_of_last[...] = jnp.dot(flat, table[...], preferred_element_type=jnp.float32)

        @pl.when(i > 0)
        def _():
            for j in range(COPIES):
                send(i - 1, j).start()

        return carry

    lax.fori_loop(0, STEPS, body, 0)
    finish(spectra_of_last[...], STEPS - 1)
    for j in range(COPIES):
        send(STEPS - 1, j).start()
    for i in range(STEPS):
        for j in range(COPIES):
            send(i, j).wait()


def whiten(signals, kept_bins):
    hbm = pl.BlockSpec(memory_space=pltpu.HBM)
    return pl.pallas_call(
        whiten_kernel,
        in_specs=[hbm, hbm, hbm],
        out_specs=hbm,
        out_shape=jax.ShapeDtypeStruct((KEPT, COPIES, LOCAL, WIDE), jnp.bfloat16),
        scratch_shapes=[
            pltpu.SMEM((KEPT,), jnp.int32),
            pltpu.VMEM((SAMPLES, 2 * CAND), jnp.bfloat16),
            pltpu.VMEM((STEPS, LOCAL, SPAN, SAMPLES), jnp.bfloat16),
            pltpu.VMEM((KEPT, CAND), jnp.float32),
            pltpu.VMEM((LOCAL * SPAN, 2 * CAND), jnp.float32),
            pltpu.VMEM((KEPT * LOCAL, LANES), jnp.float32),
            pltpu.VMEM((STEPS, KEPT, LOCAL, LANES), jnp.bfloat16),
            pltpu.SemaphoreType.DMA((2,)),
            pltpu.SemaphoreType.DMA((STEPS,)),
            pltpu.SemaphoreType.DMA((STEPS, COPIES)),
        ],
        compiler_params=pltpu.CompilerParams(vmem_limit_bytes=60 * 1024 * 1024),
        name="whiten",
    )(kept_bins, build_table(), jnp.transpose(signals, (1, 2, 0)))


def ranks(block_of, which):
    member = (block_of == which).reshape(GROUPS, GROUP)
    index = np.arange(GROUP)
    before = jnp.asarray((index[:, None] < index[None, :]).astype(jnp.bfloat16))
    ones = member.astype(jnp.bfloat16)
    rank = jnp.dot(ones, before, preferred_element_type=jnp.float32).astype(jnp.int32)
    count = jnp.sum(member.astype(jnp.int32), axis=1)
    group = np.arange(GROUPS)
    earlier = jnp.asarray((group[:, None] < group[None, :]).astype(np.int32))
    offset = jnp.sum(count[:, None] * earlier, axis=0)
    return member, rank, count, offset


def places(block_of, row, col):
    member, rank, count, offset = ranks(block_of, row)
    col_member, col_rank, _, col_offset = ranks(block_of, col)
    shift, col_shift = offset % 16, col_offset % 16
    second = jnp.where(row == col, 0, (shift + count) // 16 * 16 + 16)
    col_target = jnp.where(col_member, col_rank + (second + col_shift)[:, None], -1)
    target = jnp.where(member, rank + shift[:, None], col_target)
    return target, jnp.stack([offset - shift, col_offset - col_shift, second])


def cross_kernel(
    base_ref, target_ref, panel_ref, real_hbm, imag_hbm, sorted_rows, sorted_cols, both, out, sems
):
    place = lax.broadcasted_iota(jnp.int32, (PAIR, GROUP), 0)
    sides = (sorted_rows, sorted_cols)
    for dest in sides:
        dest[0:16, :] = jnp.zeros((16, WIDE), jnp.bfloat16)
    both[:, PAIR:, :] = jnp.zeros((2, WINDOW, WIDE), jnp.bfloat16)
    for g in range(GROUPS):
        group = panel_ref[g * GROUP : (g + 1) * GROUP, :]
        hit = (place == target_ref[g : g + 1, :]).astype(jnp.bfloat16)
        slot = g % 2
        both[slot, 0:PAIR, :] = jnp.dot(hit, group, preferred_element_type=jnp.float32).astype(
            jnp.bfloat16
        )
        for side, dest in enumerate(sides):
            start = pl.multiple_of(base_ref[2, g], 16) if side else 0
            base = pl.multiple_of(base_ref[side, g], 16)
            dest[pl.ds(base, 16), :] += both[slot, pl.ds(start, 16), :]
            dest[pl.ds(pl.multiple_of(base + 16, 16), GROUP), :] = both[
                slot, pl.ds(pl.multiple_of(start + 16, 16), GROUP), :
            ]

    cols = sorted_cols[0:HALF, :]
    scale = 1.0 / WINDOWS

    def send(i, part):
        span = pl.ds(i * ROW_TILE, ROW_TILE)
        dest = (real_hbm, imag_hbm)[part].at[0, span]
        return pltpu.make_async_copy(out.at[i, part], dest, sems.at[i, part])

    for i in range(HALF // ROW_TILE):
        rows = sorted_rows[i * ROW_TILE : (i + 1) * ROW_TILE, :]
        halves = [rows[:, k * SPAN : (k + 1) * SPAN] for k in range(2 * STEPS)]
        turned = [(halves[2 * k + 1], -halves[2 * k]) for k in range(STEPS)]
        twisted = jnp.concatenate([half for pair in turned for half in pair], axis=1)
        for part, left in enumerate((rows, twisted)):
            total = lax.dot_general(left, cols, NT, preferred_element_type=jnp.float32)
            out[i, part] = (total * scale).astype(jnp.bfloat16)
            send(i, part).start()
    for i in range(HALF // ROW_TILE):
        for part in range(2):
            send(i, part).wait()


def cross(base, target, panel):
    shape = jax.ShapeDtypeStruct((1, HALF, HALF), jnp.bfloat16)
    hbm = pl.BlockSpec(memory_space=pltpu.HBM)
    vmem = pl.BlockSpec(memory_space=pltpu.VMEM)
    return pl.pallas_call(
        cross_kernel,
        in_specs=[pl.BlockSpec(memory_space=pltpu.SMEM), vmem, vmem],
        out_specs=[hbm, hbm],
        out_shape=[shape, shape],
        scratch_shapes=[
            pltpu.VMEM((HALF + WINDOW, WIDE), jnp.bfloat16),
            pltpu.VMEM((HALF + WINDOW, WIDE), jnp.bfloat16),
            pltpu.VMEM((2, PAIR + WINDOW, WIDE), jnp.bfloat16),
            pltpu.VMEM((HALF // ROW_TILE, 2, ROW_TILE, HALF), jnp.bfloat16),
            pltpu.SemaphoreType.DMA((HALF // ROW_TILE, 2)),
        ],
        compiler_params=pltpu.CompilerParams(vmem_limit_bytes=32 * 1024 * 1024),
        name="cross",
    )(base, target, panel)


def on_device(signals, block_of, kept_bins):
    panels = whiten(signals, kept_bins).reshape(KEPT * COPIES, LOCAL, WIDE)
    relaid = lax.all_to_all(
        panels, ("freq", "row", "col"), split_axis=0, concat_axis=0, tiled=True
    )
    target, base = places(block_of, lax.axis_index("row"), lax.axis_index("col"))
    cross_real, cross_imag = cross(base, target, relaid.reshape(STATIONS, WIDE))
    return (cross_real, cross_imag)


def solution(mesh):
    return jax.shard_map(
        on_device,
        mesh=mesh,
        in_specs=(P(None, ("freq", "row", "col"), None), P(), P()),
        out_specs=(P("freq", "row", "col"), P("freq", "row", "col")),
        check_vma=False,
    )
```

```python
import math

import jax
import jax.numpy as jnp
import numpy as np
from jax import lax
from jax.experimental import pallas as pl
from jax.experimental.pallas import tpu as pltpu
from jax.sharding import PartitionSpec as P

STATIONS = 2048
SAMPLES = 2000
FIRST = 40
CAND = 128
WINDOWS = 320
KEPT = 32
LOCAL = 16
WIDE = 2 * WINDOWS
COPIES = 4
HALF = STATIONS // 2
GROUP = 256
GROUPS = STATIONS // GROUP
WINDOW = GROUP + 16
PAIR = GROUP + 48
SPAN = 64
STEPS = WINDOWS // SPAN
DEPTH = 2
ROW_TILE = 128
LANES = 128
NT = (((1,), (1,)), ((), ()))


def build_table():
    turns = np.arange(SAMPLES)[:, None] * (np.arange(CAND) + FIRST)[None, :] % SAMPLES
    angle = turns.astype(np.float32) * np.float32(2.0 * math.pi / SAMPLES)
    return np.concatenate([np.cos(angle), -np.sin(angle)], axis=1).astype(jnp.bfloat16)


def bin_order(kept, chosen):
    lane = lax.broadcasted_iota(jnp.int32, (1, CAND), 1)
    for b in range(KEPT):
        chosen[pl.ds(b, 1), :] = (lane == kept[b]).astype(jnp.float32)
    first = chosen[...]
    other = 1.0 - jnp.sum(first, axis=0, keepdims=True)
    square = (CAND, CAND)
    before = lax.broadcasted_iota(jnp.int32, square, 0) < lax.broadcasted_iota(jnp.int32, square, 1)
    rank = jnp.dot(
        jnp.broadcast_to(other, (8, CAND)).astype(jnp.bfloat16),
        before.astype(jnp.bfloat16),
        preferred_element_type=jnp.float32,
    )[:1]
    place = jnp.where(other > 0.5, rank, -1.0).astype(jnp.int32)
    rest = lax.broadcasted_iota(jnp.int32, (CAND - KEPT, CAND), 0) == place
    rest = rest.astype(jnp.float32)
    none_first, none_rest = jnp.zeros_like(first), jnp.zeros_like(rest)
    halves = ((first, none_first), (none_first, first), (rest, none_rest), (none_rest, rest))
    order = jnp.concatenate([jnp.concatenate(pair, axis=1) for pair in halves], axis=0)
    return order.astype(jnp.bfloat16)


def whiten_kernel(
    kept_hbm,
    table_hbm,
    signals_hbm,
    out_hbm,
    kept,
    table,
    signals,
    chosen,
    spectra_of_last,
    rows,
    panels,
    small_sems,
    sems,
    out_sems,
):
    def fetch(i):
        span = pl.ds(pl.multiple_of(i * SPAN, SPAN), SPAN)
        return pltpu.make_async_copy(signals_hbm.at[:, span], signals.at[i], sems.at[i])

    def send(i, j):
        lanes = pl.ds(pl.multiple_of(i * LANES, LANES), LANES)
        return pltpu.make_async_copy(
            panels.at[i], out_hbm.at[:, j, :, lanes], out_sems.at[i, j]
        )

    kept_copy = pltpu.make_async_copy(kept_hbm, kept, small_sems.at[0])
    table_copy = pltpu.make_async_copy(table_hbm, table, small_sems.at[1])
    kept_copy.start()
    table_copy.start()
    fetch(0).start()
    kept_copy.wait()
    order = bin_order(kept, chosen)
    table_copy.wait()
    fetch(1).start()
    table[...] = lax.dot_general(
        table[...], order, NT, preferred_element_type=jnp.float32
    ).astype(jnp.bfloat16)
    low = lax.broadcasted_iota(jnp.int32, (KEPT, LANES), 1) < SPAN

    def finish(spectra, i):
        band_power = jnp.sum(spectra * spectra, axis=1, keepdims=True) * (1.0 / CAND)
        scale = lax.rsqrt(band_power + 1e-06)
        picked = (spectra[:, :LANES] * scale).astype(jnp.bfloat16).T[: 2 * KEPT]
        picked = picked.astype(jnp.float32)
        for pair in range(LOCAL // 2):
            real = picked[:KEPT, pair * LANES : (pair + 1) * LANES]
            imag = picked[KEPT:, pair * LANES : (pair + 1) * LANES]
            even = jnp.where(low, real, pltpu.roll(imag, SPAN, 1))
            odd = jnp.where(low, pltpu.roll(real, SPAN, 1), imag)
            rows[pl.Slice(2 * pair, KEPT, LOCAL), :] = even
            rows[pl.Slice(2 * pair + 1, KEPT, LOCAL), :] = odd
        panels[i] = rows[...].reshape(KEPT, LOCAL, LANES).astype(jnp.bfloat16)

    spectra_of_last[...] = jnp.zeros_like(spectra_of_last)

    def body(i, carry):
        fetch(i).wait()

        @pl.when(i + DEPTH < STEPS)
        def _():
            fetch(i + DEPTH).start()

        finish(spectra_of_last[...], jnp.maximum(i - 1, 0))
        flat = signals[i].reshape(LOCAL * SPAN, SAMPLES)
        spectra_of_last[...] = jnp.dot(flat, table[...], preferred_element_type=jnp.float32)

        @pl.when(i > 0)
        def _():
            for j in range(COPIES):
                send(i - 1, j).start()

        return carry

    lax.fori_loop(0, STEPS, body, 0)
    finish(spectra_of_last[...], STEPS - 1)
    for j in range(COPIES):
        send(STEPS - 1, j).start()
    for i in range(STEPS):
        for j in range(COPIES):
            send(i, j).wait()


def whiten(signals, kept_bins):
    hbm = pl.BlockSpec(memory_space=pltpu.HBM)
    return pl.pallas_call(
        whiten_kernel,
        in_specs=[hbm, hbm, hbm],
        out_specs=hbm,
        out_shape=jax.ShapeDtypeStruct((KEPT, COPIES, LOCAL, WIDE), jnp.bfloat16),
        scratch_shapes=[
            pltpu.SMEM((KEPT,), jnp.int32),
            pltpu.VMEM((SAMPLES, 2 * CAND), jnp.bfloat16),
            pltpu.VMEM((STEPS, LOCAL, SPAN, SAMPLES), jnp.bfloat16),
            pltpu.VMEM((KEPT, CAND), jnp.float32),
            pltpu.VMEM((LOCAL * SPAN, 2 * CAND), jnp.float32),
            pltpu.VMEM((KEPT * LOCAL, LANES), jnp.float32),
            pltpu.VMEM((STEPS, KEPT, LOCAL, LANES), jnp.bfloat16),
            pltpu.SemaphoreType.DMA((2,)),
            pltpu.SemaphoreType.DMA((STEPS,)),
            pltpu.SemaphoreType.DMA((STEPS, COPIES)),
        ],
        compiler_params=pltpu.CompilerParams(vmem_limit_bytes=60 * 1024 * 1024),
        name="whiten",
    )(kept_bins, build_table(), jnp.transpose(signals, (1, 2, 0)))


def ranks(block_of, which):
    member = (block_of == which).reshape(GROUPS, GROUP)
    index = np.arange(GROUP)
    before = jnp.asarray((index[:, None] < index[None, :]).astype(jnp.bfloat16))
    ones = member.astype(jnp.bfloat16)
    rank = jnp.dot(ones, before, preferred_element_type=jnp.float32).astype(jnp.int32)
    count = jnp.sum(member.astype(jnp.int32), axis=1)
    group = np.arange(GROUPS)
    earlier = jnp.asarray((group[:, None] < group[None, :]).astype(np.int32))
    offset = jnp.sum(count[:, None] * earlier, axis=0)
    return member, rank, count, offset


def places(block_of, row, col):
    member, rank, count, offset = ranks(block_of, row)
    col_member, col_rank, _, col_offset = ranks(block_of, col)
    shift, col_shift = offset % 16, col_offset % 16
    second = jnp.where(row == col, 0, (shift + count) // 16 * 16 + 16)
    col_target = jnp.where(col_member, col_rank + (second + col_shift)[:, None], -1)
    target = jnp.where(member, rank + shift[:, None], col_target)
    return target, jnp.stack([offset - shift, col_offset - col_shift, second])


def cross_kernel(
    base_ref, target_ref, panel_ref, real_hbm, imag_hbm, sorted_rows, sorted_cols, both, out, sems
):
    place = lax.broadcasted_iota(jnp.int32, (PAIR, GROUP), 0)
    sides = (sorted_rows, sorted_cols)
    for dest in sides:
        dest[0:16, :] = jnp.zeros((16, WIDE), jnp.bfloat16)
    both[:, PAIR:, :] = jnp.zeros((2, WINDOW, WIDE), jnp.bfloat16)
    for g in range(GROUPS):
        group = panel_ref[g * GROUP : (g + 1) * GROUP, :]
        hit = (place == target_ref[g : g + 1, :]).astype(jnp.bfloat16)
        slot = g % 2
        both[slot, 0:PAIR, :] = jnp.dot(hit, group, preferred_element_type=jnp.float32).astype(
            jnp.bfloat16
        )
        for side, dest in enumerate(sides):
            start = pl.multiple_of(base_ref[2, g], 16) if side else 0
            base = pl.multiple_of(base_ref[side, g], 16)
            dest[pl.ds(base, 16), :] += both[slot, pl.ds(start, 16), :]
            dest[pl.ds(pl.multiple_of(base + 16, 16), GROUP), :] = both[
                slot, pl.ds(pl.multiple_of(start + 16, 16), GROUP), :
            ]

    cols = sorted_cols[0:HALF, :]
    scale = 1.0 / WINDOWS

    def send(i, part):
        span = pl.ds(i * ROW_TILE, ROW_TILE)
        dest = (real_hbm, imag_hbm)[part].at[0, span]
        return pltpu.make_async_copy(out.at[i, part], dest, sems.at[i, part])

    for i in range(HALF // ROW_TILE):
        rows = sorted_rows[i * ROW_TILE : (i + 1) * ROW_TILE, :]
        halves = [rows[:, k * SPAN : (k + 1) * SPAN] for k in range(2 * STEPS)]
        turned = [(halves[2 * k + 1], -halves[2 * k]) for k in range(STEPS)]
        twisted = jnp.concatenate([half for pair in turned for half in pair], axis=1)
        total = lax.dot_general(
            jnp.concatenate([rows, twisted], axis=0), cols, NT, preferred_element_type=jnp.float32
        )
        for part in range(2):
            mine = total[part * ROW_TILE : (part + 1) * ROW_TILE]
            out[i, part] = (mine * scale).astype(jnp.bfloat16)
            send(i, part).start()
    for i in range(HALF // ROW_TILE):
        for part in range(2):
            send(i, part).wait()


def cross(base, target, panel):
    shape = jax.ShapeDtypeStruct((1, HALF, HALF), jnp.bfloat16)
    hbm = pl.BlockSpec(memory_space=pltpu.HBM)
    vmem = pl.BlockSpec(memory_space=pltpu.VMEM)
    return pl.pallas_call(
        cross_kernel,
        in_specs=[pl.BlockSpec(memory_space=pltpu.SMEM), vmem, vmem],
        out_specs=[hbm, hbm],
        out_shape=[shape, shape],
        scratch_shapes=[
            pltpu.VMEM((HALF + WINDOW, WIDE), jnp.bfloat16),
            pltpu.VMEM((HALF + WINDOW, WIDE), jnp.bfloat16),
            pltpu.VMEM((2, PAIR + WINDOW, WIDE), jnp.bfloat16),
            pltpu.VMEM((HALF // ROW_TILE, 2, ROW_TILE, HALF), jnp.bfloat16),
            pltpu.SemaphoreType.DMA((HALF // ROW_TILE, 2)),
        ],
        compiler_params=pltpu.CompilerParams(vmem_limit_bytes=32 * 1024 * 1024),
        name="cross",
    )(base, target, panel)


def on_device(signals, block_of, kept_bins):
    panels = whiten(signals, kept_bins).reshape(KEPT * COPIES, LOCAL, WIDE)
    relaid = lax.all_to_all(
        panels, ("freq", "row", "col"), split_axis=0, concat_axis=0, tiled=True
    )
    target, base = places(block_of, lax.axis_index("row"), lax.axis_index("col"))
    cross_real, cross_imag = cross(base, target, relaid.reshape(STATIONS, WIDE))
    return (cross_real, cross_imag)


def solution(mesh):
    return jax.shard_map(
        on_device,
        mesh=mesh,
        in_specs=(P(None, ("freq", "row", "col"), None), P(), P()),
        out_specs=(P("freq", "row", "col"), P("freq", "row", "col")),
        check_vma=False,
    )
```
